32 devices in a mesh: dp: 8 (over y, x, core), tensor: 4 (over z).
Axes of the slice: x: 2, y: 2, z: 4, core: 2. Of those that a mesh axis runs over, the one named last changes fastest.
Arguments:
- hidden_state_input: bfloat16 [4096, 3584], P(('dp', 'tensor')), may hold values from -500 to 500
- token_embedding_input: bfloat16 [4096, 3584], P(('dp', 'tensor')), may hold values from -500 to 500
- input_norm_gain: float32 [7168], replicated, may hold values from 0.1 to 1.9
- query_projection_weight: bfloat16 [7168, 3584], P('dp', 'tensor'), may hold values from -0.0625 to 0.0625
- key_projection_weight: bfloat16 [7168, 3584], P('dp', 'tensor'), may hold values from -0.0625 to 0.0625
- value_projection_weight: bfloat16 [7168, 3584], P('dp', 'tensor'), may hold values from -0.0625 to 0.0625
- adapter_down_maps: bfloat16 [7168, 384], replicated, may hold values from -1 to 1
- adapter_up_maps: bfloat16 [3, 128, 3584], P(None, None, 'tensor'), may hold values from -2 to 2
- output_projection_weight: bfloat16 [3584, 3584], P('tensor'), may hold values from -0.09375 to 0.09375
- segment: int32 [4096], P('dp'), may hold values from 0 to 3, as said below
- live_token_length: int32 [8], P('dp'), may hold values from 256 to 512, as said below
- request_cache_row: int32 [32], P('dp'), may hold values from 0 to 31, as said below
Outputs:
- block_out: bfloat16 [4096, 3584], P(('dp', 'tensor'))
- kv_cache: bfloat16 [32, 128, 2, 3584], P(None, 'dp', None, 'tensor')
The draws below stay inside these ranges and needn't reach their ends.
Inputs may be any that keep to these rules, and one draw needn't show every extreme that they name: `segment`: within a stream, the live slots carry request numbers that never fall, every request 0 to 3 appears, each on (129) // 2 to 128 slots, some request in every draw on exactly 128; slots at or past live_token_length hold 3. `live_token_length`: each stream's live tokens; some stream is full in every draw. `request_cache_row`: A permutation of the 32 cache rows.
All inputs are finite; a program needn't handle non-finite values.
Results may differ from the reference program's by a relative error of at most 0.015.
The reference program's roundings to bfloat16 on the way count: a program that leaves them out, or rounds other values in their place, can miss the bound.
Values may be sent and summed in bfloat16 or wider, within the bound.
A program may use at most 128 MiB of HBM per device.

```python
import math
import jax
import jax.numpy as jnp
from jax import lax

DM = 3584
DIN = 7168
HD = 224
ADAPTER_RANK = 128
HEADS = 16
R_DEV = 4
STREAM = 512
LMAX = 128
TOKENS = 4096
REQS = 32
N_DP = 8
N_TENSOR = 4


def adapter_down_complete(key):
    first_key = jax.random.fold_in(jax.random.fold_in(key, 11), 0)
    base = jnp.clip(jax.random.normal(first_key, (DIN, 3 * ADAPTER_RANK), jnp.float32), -5.0, 5.0)
    return base / math.sqrt(DIN)


def input_half(key, half):
    noise_key, column_key = jax.random.split(jax.random.fold_in(key, 101 + half), 2)
    row_scale = jnp.exp(jax.random.uniform(jax.random.fold_in(key, 99), (TOKENS, 1), jnp.float32) * math.log(10.0))
    column_scale = jnp.exp(jax.random.uniform(column_key, (1, DM), jnp.float32) * math.log(10.0))
    noise = jnp.clip(jax.random.normal(noise_key, (TOKENS, DM), jnp.float32), -4.0, 4.0)
    drawn = noise * row_scale * column_scale
    return drawn.astype(jnp.bfloat16)


def draw_hidden_state_input(key, part):
    return input_half(key, 0)


def draw_token_embedding_input(key, part):
    return input_half(key, 1)


def draw_adapter_down_maps(key, part):
    return adapter_down_complete(key).astype(jnp.bfloat16)


def draw_adapter_up_maps(key, part):
    first_key = jax.random.fold_in(jax.random.fold_in(key, 13), 0)
    base = jnp.clip(jax.random.normal(first_key, (3, ADAPTER_RANK, HEADS * HD), jnp.float32), -5.0, 5.0)
    return (base / math.sqrt(ADAPTER_RANK)).astype(jnp.bfloat16)


def stream_lengths(key):
    groups = REQS // R_DEV
    length_key, full_key = jax.random.split(jax.random.fold_in(key, 7))
    lengths = jax.random.randint(length_key, (groups, R_DEV), (LMAX + 1) // 2, LMAX + 1)
    full_stream = jax.random.randint(full_key, (), 0, groups)
    lengths = jnp.where(jnp.arange(groups)[:, None] == full_stream, LMAX, lengths)
    return lengths.astype(jnp.int32)


def draw_live_token_length(key, part):
    return jnp.sum(stream_lengths(key), axis=1).astype(jnp.int32)


def draw_segment(key, part):
    lengths = stream_lengths(key)
    ends = jnp.cumsum(lengths, axis=1)
    place = jnp.arange(STREAM, dtype=jnp.int32)
    numbers = jnp.sum((place[None, :, None] >= ends[:, None, :]).astype(jnp.int32), axis=-1)
    numbers = jnp.minimum(numbers, R_DEV - 1)
    return numbers.reshape(TOKENS).astype(jnp.int32)


def draw_request_cache_row(key, part):
    return jax.random.permutation(jax.random.fold_in(key, 31), REQS).astype(jnp.int32)


def levels(stream_key, dims, cuts, least, top_value):
    loudness, own = 1.0, jax.random.fold_in(stream_key, 6)
    for dim, shards_of in cuts:
        draws = jnp.exp(jax.random.uniform(jax.random.fold_in(own, dim), (shards_of,), jnp.float32, least / len(cuts), top_value / len(cuts)))
        loudness = loudness * jnp.repeat(draws, dims[dim] // shards_of).reshape([-1 if axis == dim else 1 for axis in range(len(dims))])
    return loudness


def bell_draw(own_key, dims, spread, most, shards=(), held_as=jnp.bfloat16):
    drawn = spread * jax.random.normal(own_key, dims, jnp.float32)
    if shards:
        drawn = drawn * levels(own_key, dims, shards, -0.22, 0.18)
    return jnp.clip(drawn, -most, most).astype(held_as)


def setup_inputs(seed: int = 0) -> dict:
    seeds = jax.random.split(jax.random.key(seed), 13)
    hidden_state_input = draw_hidden_state_input(jax.random.fold_in(seeds[12], 71), 0)
    token_embedding_input = draw_token_embedding_input(jax.random.fold_in(seeds[12], 71), 0)
    input_norm_gain = jnp.clip(1.0 + 0.18 * jax.random.normal(seeds[2], (DIN,), jnp.float32), 0.1, 1.9)
    query_projection_weight = bell_draw(seeds[3], (DIN, HEADS * HD), DIN ** -0.5, 0.0625, ((0, 8), (1, 4)))
    key_projection_weight = bell_draw(seeds[4], (DIN, HEADS * HD), DIN ** -0.5, 0.0625, ((0, 8), (1, 4)))
    value_projection_weight = bell_draw(seeds[5], (DIN, HEADS * HD), DIN ** -0.5, 0.0625, ((0, 8), (1, 4)))
    adapter_down_maps = draw_adapter_down_maps(jax.random.fold_in(seeds[12], 71), 0)
    adapter_up_maps = draw_adapter_up_maps(jax.random.fold_in(seeds[12], 71), 0)
    output_projection_weight = bell_draw(seeds[8], (HEADS * HD, DM), (HEADS * HD) ** -0.5, 0.09375, ((0, 4),))
    segment = draw_segment(jax.random.fold_in(seeds[12], 71), 0)
    live_token_length = draw_live_token_length(jax.random.fold_in(seeds[12], 71), 0)
    request_cache_row = draw_request_cache_row(jax.random.fold_in(seeds[12], 71), 0)
    return dict(hidden_state_input=hidden_state_input, token_embedding_input=token_embedding_input, input_norm_gain=input_norm_gain, query_projection_weight=query_projection_weight, key_projection_weight=key_projection_weight, value_projection_weight=value_projection_weight, adapter_down_maps=adapter_down_maps, adapter_up_maps=adapter_up_maps, output_projection_weight=output_projection_weight, segment=segment, live_token_length=live_token_length, request_cache_row=request_cache_row)


def reference(hidden_state_input, token_embedding_input, input_norm_gain, query_projection_weight, key_projection_weight, value_projection_weight, adapter_down_maps, adapter_up_maps, output_projection_weight, segment, live_token_length, request_cache_row):
    hidden_streams = hidden_state_input.reshape(N_DP, STREAM, DM)
    embed_streams = token_embedding_input.reshape(N_DP, STREAM, DM)
    segment_streams = segment.reshape(N_DP, STREAM)
    group_cols = HEADS * HD // N_TENSOR

    def one_stream(operands):
        hidden_part, embed_part, segment_part, live = operands
        combined = jnp.concatenate([hidden_part, embed_part], 1).astype(jnp.float32)
        factor = lax.rsqrt(lax.optimization_barrier(jnp.mean(combined * combined, axis=1, keepdims=True)) + 1e-05)
        normalized_hidden = (combined * factor * input_norm_gain).astype(jnp.bfloat16)
        adapter_update = jnp.dot(normalized_hidden, adapter_down_maps, preferred_element_type=jnp.float32).astype(jnp.bfloat16)
        projected = []
        for adapter_selector, weight in enumerate((query_projection_weight, key_projection_weight, value_projection_weight)):
            token_total = jnp.dot(normalized_hidden, weight, preferred_element_type=jnp.float32)
            token_total = token_total + jnp.dot(adapter_update[:, adapter_selector * ADAPTER_RANK:(adapter_selector + 1) * ADAPTER_RANK], adapter_up_maps[adapter_selector], preferred_element_type=jnp.float32)
            projected.append(token_total.astype(jnp.bfloat16))
        query, keys, values = projected
        position = jnp.arange(STREAM, dtype=jnp.int32)
        query_heads = query.reshape(STREAM, HEADS, HD).astype(jnp.float32)
        key_heads = keys.reshape(STREAM, HEADS, HD).astype(jnp.float32)
        value_heads = values.reshape(STREAM, HEADS, HD).astype(jnp.float32)
        scores = jnp.einsum('qhd,khd->hqk', query_heads, key_heads) / math.sqrt(HD)
        allowed = (segment_part[:, None] == segment_part[None, :]) & (position[None, :] <= position[:, None]) & (position[None, :] < live)
        scores = jnp.where(allowed[None], scores, -1e+30)
        top = lax.optimization_barrier(jnp.max(scores, axis=-1, keepdims=True))
        expo = jnp.exp(scores - top)
        weights = (expo / lax.optimization_barrier(jnp.sum(expo, axis=-1, keepdims=True))).astype(jnp.bfloat16)
        mixed = jnp.einsum('hqk,khd->qhd', weights.astype(jnp.float32), value_heads)
        mixed = jnp.where((position < live)[:, None, None], mixed, 0.0)
        attended = mixed.astype(jnp.bfloat16).reshape(STREAM, HEADS * HD)
        grouped = attended.reshape(STREAM, N_TENSOR, group_cols).astype(jnp.float32)
        out_groups = output_projection_weight.reshape(N_TENSOR, group_cols, DM).astype(jnp.float32)
        partial_value = jnp.einsum('stc,tcd->tsd', grouped, out_groups).astype(jnp.bfloat16)
        result = lax.optimization_barrier(jnp.sum(partial_value.astype(jnp.float32), axis=0)).astype(jnp.bfloat16)
        membership = ((segment_part[:, None] == jnp.arange(R_DEV, dtype=jnp.int32)[None, :]) & (position < live)[:, None]).astype(jnp.int32)
        lengths = lax.optimization_barrier(jnp.sum(membership, axis=0))
        starts = jnp.cumsum(lengths) - lengths
        offsets = jnp.arange(LMAX, dtype=jnp.int32)
        source = jnp.minimum(starts[:, None] + offsets[None, :], STREAM - 1).astype(jnp.int32)
        alive = offsets[None, :] < lengths[:, None]
        stacked = jnp.stack([keys, values], 1)
        taken = jnp.take(stacked, source.reshape(-1), axis=0).reshape(R_DEV, LMAX, 2, HEADS * HD)
        taken = jnp.where(alive[:, :, None, None], taken, jnp.zeros((), taken.dtype))
        return (result, taken)
    outputs, requests = lax.map(one_stream, (hidden_streams, embed_streams, segment_streams, live_token_length))
    block_out = outputs.reshape(TOKENS, DM)
    kv_cache = jnp.zeros((REQS, LMAX, 2, HEADS * HD), requests.dtype).at[request_cache_row].set(requests.reshape(REQS, LMAX, 2, HEADS * HD))
    return (block_out, kv_cache)
```

```python
import functools
import math

import jax
import jax.numpy as jnp
from jax import lax
from jax.experimental import pallas as pl
from jax.experimental.pallas import tpu as pltpu
from jax.sharding import PartitionSpec as P

HD = 224


BF = jnp.bfloat16
F32 = jnp.float32
MESH = pl.DeviceIdType.MESH


def flip(d, r):
    return sum(b * ((d // b + r // b) % 2) for b in (1, 2, 4))


def project_kernel(
    depth,
    n_z,
    din,
    x_ref,
    wk_ref,
    wv_ref,
    wq_ref,
    up_ref,
    kv_ref,
    q_ref,
    xs,
    ws,
    acc,
    loc_sem,
    x_send,
    x_recv,
    own_send,
    own_recv,
    fwd_send,
    fwd_recv,
    sib_send,
    sib_recv,
):
    d = lax.axis_index("dp")
    z = lax.axis_index("tensor")
    near = (flip(d, 2), flip(d, 4))
    sib = flip(d, 1)
    cols = wk_ref.shape[1]
    half = depth // 2
    mats = (wk_ref, wv_ref, wq_ref)
    has_left, has_right = z > 0, z < n_z - 1

    barrier = pltpu.get_barrier_semaphore()
    for other in near + (sib,):
        pl.semaphore_signal(barrier, inc=1, device_id=(other, z), device_id_type=MESH)

    @pl.when(has_left)
    def _():
        pl.semaphore_signal(barrier, inc=1, device_id=(d, z - 1), device_id_type=MESH)

    @pl.when(has_right)
    def _():
        pl.semaphore_signal(barrier, inc=1, device_id=(d, z + 1), device_id_type=MESH)

    at_end = (z == 0) | (z == n_z - 1)

    @pl.when(at_end)
    def _():
        pl.semaphore_wait(barrier, 4)

    @pl.when(jnp.logical_not(at_end))
    def _():
        pl.semaphore_wait(barrier, 5)

    def remote(src, dst, send, recv, target):
        return pltpu.make_async_remote_copy(
            src_ref=src,
            dst_ref=dst,
            send_sem=send,
            recv_sem=recv,
            device_id=target,
            device_id_type=MESH,
        )

    def token_copy(way, step):
        src_z = z - step if way == 0 else z + step
        to_z = z + 1 if way == 0 else z - 1
        src = x_ref if step == 0 else xs.at[jnp.clip(src_z, 0, n_z - 1)]
        return remote(
            src,
            xs.at[jnp.clip(src_z, 0, n_z - 1)],
            x_send.at[way, step],
            x_recv.at[way, step],
            (d, jnp.clip(to_z, 0, n_z - 1)),
        )

    def token_sends(way, step):
        if way == 0:
            return (z - step >= 0) & has_right
        return (z + step <= n_z - 1) & has_left

    def token_start(step):
        for way in (0, 1):

            @pl.when(token_sends(way, step))
            def _():
                token_copy(way, step).start()

    def token_wait_recv(step):
        for way in (0, 1):
            arrives = (z - step - 1 >= 0) if way == 0 else (z + step + 1 <= n_z - 1)

            @pl.when(arrives)
            def _():
                src_z = z - step - 1 if way == 0 else z + step + 1
                slot = xs.at[jnp.clip(src_z, 0, n_z - 1)]
                remote(
                    slot, slot, x_send.at[way, step], x_recv.at[way, step], (sib, z)
                ).wait_recv()

    def token_wait_send(step):
        for way in (0, 1):

            @pl.when(token_sends(way, step))
            def _():
                token_copy(way, step).wait_send()

    def block(r, m):
        return ws.at[r, :, pl.ds(m * cols, cols)]

    def part(r, m, h):
        return ws.at[r, pl.ds(h * half, half), pl.ds(m * cols, cols)]

    def own_copy(m, a, h):
        return remote(
            mats[m].at[pl.ds(h * half, half), :],
            part(2 << a, m, h),
            own_send.at[m, a, h],
            own_recv.at[m, a, h],
            (near[a], z),
        )

    def own_start(m):
        for first in (0, 1):
            for a in (0, 1):
                own_copy(m, a, a if first == 0 else 1 - a).start()

    def fwd_copy(m, a):
        h = a
        return remote(
            part(2 << a, m, h),
            part(6, m, h),
            fwd_send.at[m, a],
            fwd_recv.at[m, a],
            (near[1 - a], z),
        )

    def fwd_recv_wait(m, a):
        remote(
            part(6, m, a), part(6, m, a), fwd_send.at[m, a], fwd_recv.at[m, a], (sib, z)
        ).wait_recv()

    def sib_copy(m, j):
        src = mats[m] if j == 0 else block(2 * j, m)
        return remote(src, block(2 * j + 1, m), sib_send.at[m, j], sib_recv.at[m, j], (sib, z))

    def local_copy(m):
        return pltpu.make_async_copy(mats[m], block(0, m), loc_sem.at[m])

    x_local = pltpu.make_async_copy(x_ref, xs.at[z], loc_sem.at[3])

    token_start(0)
    own_start(0)
    own_start(1)
    x_local.start()
    for m in range(3):
        local_copy(m).start()
    for m in range(2):
        sib_copy(m, 0).start()

    def take_own(m):
        for a in (0, 1):
            own_copy(m, a, a).wait_recv()
            fwd_copy(m, a).start()
        for a in (0, 1):
            own_copy(m, a, 1 - a).wait_recv()
            sib_copy(m, a + 1).start()

    def take_diag(m):
        for a in (0, 1):
            fwd_recv_wait(m, a)
        sib_copy(m, 3).start()

    take_own(0)
    own_start(2)
    sib_copy(2, 0).start()
    token_wait_recv(0)
    token_start(1)
    take_own(1)
    take_diag(0)
    token_wait_recv(1)
    token_start(2)
    token_wait_recv(2)
    x_local.wait()
    for m in range(3):
        local_copy(m).wait()
    take_own(2)
    take_diag(1)
    for m in range(2):
        for j in range(4):
            sib_copy(m, j).wait_recv()

    rows = q_ref.shape[0]
    rank = up_ref.shape[1]

    def tokens(r):
        at = pl.multiple_of(flip(d, r) * depth, 128)
        return xs[:, :, pl.ds(at, depth)].reshape(rows, depth)

    adapter = (1, 2, 0)

    def low(m):
        at = din + adapter[m] * rank
        return xs[:, :, at : at + rank].reshape(rows, rank)

    for m in range(2):
        for c in range(cols // 128):
            lo = m * cols + c * 128
            acc[:, pl.ds(lo, 128)] = jnp.dot(
                low(m), up_ref[adapter[m], :, c * 128 : (c + 1) * 128], preferred_element_type=F32
            )

    wide = 256

    def kv_tile(t, carry):
        at = pl.multiple_of(t * wide, 128)
        tile = pl.ds(at, wide)

        def add(r, c):
            acc[:, tile] += jnp.dot(tokens(r), ws[r, :, tile], preferred_element_type=F32)
            return c

        lax.fori_loop(0, 8, add, 0)
        kv_ref[:, tile] = acc[:, tile].astype(BF)
        return carry

    lax.fori_loop(0, 2 * cols // wide, kv_tile, 0)

    for c in range(cols // 128):
        acc[:, c * 128 : (c + 1) * 128] = jnp.dot(
            low(2), up_ref[adapter[2], :, c * 128 : (c + 1) * 128], preferred_element_type=F32
        )
    for j in range(3):
        sib_copy(2, j).wait_recv()

    def q_add(r, c):
        for lo in range(0, cols, wide):
            width = min(wide, cols - lo)
            acc[:, lo : lo + width] += jnp.dot(
                tokens(r), ws[r, :, 2 * cols + lo : 2 * cols + lo + width], preferred_element_type=F32
            )
        return c

    lax.fori_loop(0, 6, q_add, 0)
    take_diag(2)
    q_add(6, 0)
    sib_copy(2, 3).wait_recv()
    q_add(7, 0)
    q_ref[...] = acc[:, :cols].astype(BF)

    for step in range(n_z - 1):
        token_wait_send(step)
    for m in range(3):
        for a in (0, 1):
            for h in (0, 1):
                own_copy(m, a, h).wait_send()
            fwd_copy(m, a).wait_send()
        for j in range(4):
            sib_copy(m, j).wait_send()


def project(x, wq, wk, wv, up, n_z, din):
    depth, cols = wk.shape
    rows = n_z * x.shape[0]
    dma = pltpu.SemaphoreType.DMA
    hbm = pl.BlockSpec(memory_space=pl.ANY)
    vmem = pl.BlockSpec(memory_space=pltpu.VMEM)
    return pl.pallas_call(
        functools.partial(project_kernel, depth, n_z, din),
        out_shape=(
            jax.ShapeDtypeStruct((rows, 2 * cols), BF),
            jax.ShapeDtypeStruct((rows, cols), BF),
        ),
        in_specs=[hbm, hbm, hbm, hbm, vmem],
        out_specs=(vmem, vmem),
        scratch_shapes=[
            pltpu.VMEM((n_z,) + x.shape, BF),
            pltpu.VMEM((8, depth, 3 * cols), BF),
            pltpu.VMEM((rows, 2 * cols), F32),
            dma((4,)),
            dma((2, 3)),
            dma((2, 3)),
            dma((3, 2, 2)),
            dma((3, 2, 2)),
            dma((3, 2)),
            dma((3, 2)),
            dma((3, 4)),
            dma((3, 4)),
        ],
        compiler_params=pltpu.CompilerParams(
            collective_id=0, has_side_effects=True, vmem_limit_bytes=60 * 1024 * 1024
        ),
        cost_estimate=pl.CostEstimate(
            flops=6 * rows * din * cols, bytes_accessed=8 * depth * cols * 6, transcendentals=0
        ),
    )(x, wk, wv, wq, up)


epsilon = 1e-05
negative = -1e30


def normalize(hidden_state_input, token_embedding_input, input_norm_gain):
    combined = jnp.concatenate([hidden_state_input, token_embedding_input], 1).astype(jnp.float32)
    factor = lax.rsqrt(jnp.mean(combined * combined, axis=1, keepdims=True) + epsilon)
    return (combined * factor * input_norm_gain).astype(jnp.bfloat16)


def attend_block(query, keys, values, segment, position, live, first, count, key_end):
    heads = query.shape[1] // HD
    block_query = query[first : first + count].reshape(count, heads, HD)
    block_keys = keys.reshape(key_end, heads, HD)
    block_values = values.reshape(key_end, heads, HD)
    scores = jnp.einsum(
        "qhd,khd->hqk", block_query, block_keys, preferred_element_type=jnp.float32
    ) / math.sqrt(HD)
    query_at = position[first : first + count]
    allowed = (
        (segment[first : first + count, None] == segment[None, :key_end])
        & (position[None, :] <= query_at[:, None])
        & (position[None, :] < live)
    )
    scores = jnp.where(allowed[None], scores, negative)
    top = jnp.max(scores, axis=-1, keepdims=True)
    expo = jnp.exp(scores - top)
    weights = (expo / jnp.sum(expo, axis=-1, keepdims=True)).astype(jnp.bfloat16)
    mixed = jnp.einsum("hqk,khd->qhd", weights, block_values, preferred_element_type=jnp.float32)
    mixed = jnp.where((query_at < live)[:, None, None], mixed, 0.0)
    return mixed.astype(jnp.bfloat16).reshape(count, heads * HD)


def body(
    hidden_state_input,
    token_embedding_input,
    input_norm_gain,
    query_projection_weight,
    key_projection_weight,
    value_projection_weight,
    adapter_down_maps,
    adapter_up_maps,
    output_projection_weight,
    segment,
    live_token_length,
    request_cache_row,
):
    adapter_rank_width = adapter_up_maps.shape[1]
    head_cols = query_projection_weight.shape[1]
    normalized_hidden = normalize(hidden_state_input, token_embedding_input, input_norm_gain)
    adapter_update = jnp.dot(
        normalized_hidden, adapter_down_maps, preferred_element_type=jnp.float32
    ).astype(jnp.bfloat16)
    dp, n_z = lax.axis_size("dp"), lax.axis_size("tensor")
    depth = query_projection_weight.shape[0]
    if dp == 8 and n_z == 4:
        own = jnp.concatenate([normalized_hidden, adapter_update], 1)
        stacked, query = project(
            own,
            query_projection_weight,
            key_projection_weight,
            value_projection_weight,
            adapter_up_maps,
            n_z,
            dp * depth,
        )
        keys, values = stacked[:, :head_cols], stacked[:, head_cols:]
    else:
        stream_in, stream_low = (
            lax.all_gather(normalized_hidden, "tensor", axis=0, tiled=True),
            lax.all_gather(adapter_update, "tensor", axis=0, tiled=True),
        )
        pieces = (
            lax.all_gather(query_projection_weight, "dp", axis=0, tiled=True),
            lax.all_gather(key_projection_weight, "dp", axis=0, tiled=True),
            lax.all_gather(value_projection_weight, "dp", axis=0, tiled=True),
        )
        folded = tuple(
            (jnp.dot(stream_in, piece, preferred_element_type=jnp.float32) for piece in pieces)
        )
        projected = []
        for adapter_selector in range(3):
            adapter = jnp.dot(
                stream_low[
                    :,
                    adapter_selector * adapter_rank_width : (adapter_selector + 1) * adapter_rank_width,
                ],
                adapter_up_maps[adapter_selector],
                preferred_element_type=jnp.float32,
            )
            projected.append((folded[adapter_selector] + adapter).astype(jnp.bfloat16))
        query, keys, values = projected
        stacked = jnp.concatenate([keys, values], 1)
    stream = query.shape[0]
    position = jnp.arange(stream, dtype=jnp.int32)
    live = live_token_length[0]
    block = min(512, stream)
    attended_parts = []
    for block_index in range(stream // block):
        first = block_index * block
        attended_parts.append(
            attend_block(query, keys, values, segment, position, live, first, block, stream)
        )
    attended = jnp.concatenate(attended_parts, 0)
    block_out = lax.psum_scatter(
        jnp.dot(attended, output_projection_weight, preferred_element_type=jnp.float32).astype(
            jnp.bfloat16
        ),
        "tensor",
        scatter_dimension=0,
        tiled=True,
    )
    requests = request_cache_row.shape[0]
    longest = stream // requests
    groups = lax.axis_size("dp")
    piece_len = longest // groups
    numbers = jnp.arange(requests, dtype=jnp.int32)
    membership = ((segment[:, None] == numbers[None, :]) & (position < live)[:, None]).astype(
        jnp.int32
    )
    lengths = jnp.sum(membership, axis=0)
    earlier = numbers[:, None] < numbers[None, :]
    starts = jnp.sum(jnp.where(earlier, lengths[:, None], 0), axis=0)
    offsets = (
        jnp.arange(groups, dtype=jnp.int32)[:, None] * piece_len
        + jnp.arange(piece_len, dtype=jnp.int32)[None, :]
    )
    source_rows = jnp.minimum(starts[None, :, None] + offsets[:, None, :], stream - 1)
    alive_mask = offsets[:, None, :] < lengths[None, :, None]
    taken = jnp.take(stacked, source_rows.reshape(-1), axis=0)
    taken = jnp.where(alive_mask.reshape(-1)[:, None], taken, jnp.zeros((), jnp.bfloat16))
    taken = taken.reshape(groups, requests, piece_len * 2 * head_cols)
    row_send = jnp.broadcast_to(request_cache_row[None, :], (groups, requests))
    received, received_rows = (
        lax.all_to_all(taken, "dp", split_axis=0, concat_axis=0, tiled=True),
        lax.all_to_all(row_send, "dp", split_axis=0, concat_axis=0, tiled=True),
    )
    total_reqs = groups * requests
    placing = (
        received_rows.reshape(-1)[:, None] == jnp.arange(total_reqs, dtype=jnp.int32)[None, :]
    ).astype(jnp.bfloat16)
    flat_received = received.reshape(total_reqs, piece_len * 2 * head_cols)
    cache_rows = lax.dot_general(
        placing, flat_received, (((0,), (0,)), ((), ())), preferred_element_type=jnp.float32
    )
    kv_cache = cache_rows.astype(jnp.bfloat16).reshape(total_reqs, piece_len, 2, head_cols)
    return (block_out, kv_cache)


def solution(mesh):
    return jax.shard_map(
        body,
        mesh=mesh,
        in_specs=(
            P(("dp", "tensor"), None),
            P(("dp", "tensor"), None),
            P(),
            P("dp", "tensor"),
            P("dp", "tensor"),
            P("dp", "tensor"),
            P(),
            P(None, None, "tensor"),
            P("tensor", None),
            P("dp"),
            P("dp"),
            P("dp"),
        ),
        out_specs=(P(("dp", "tensor"), None), P(None, "dp", None, "tensor")),
        check_vma=False,
    )
```

```python
import functools
import math

import jax
import jax.numpy as jnp
from jax import lax
from jax.experimental import pallas as pl
from jax.experimental.pallas import tpu as pltpu
from jax.sharding import PartitionSpec as P

HD = 224


BF = jnp.bfloat16
F32 = jnp.float32
MESH = pl.DeviceIdType.MESH


def flip(d, r):
    return sum(b * ((d // b + r // b) % 2) for b in (1, 2, 4))


def project_kernel(
    depth,
    n_z,
    din,
    x_ref,
    wk_ref,
    wv_ref,
    wq_ref,
    up_ref,
    kv_ref,
    q_ref,
    xs,
    ws,
    acc,
    loc_sem,
    x_send,
    x_recv,
    own_send,
    own_recv,
    fwd_send,
    fwd_recv,
    sib_send,
    sib_recv,
):
    d = lax.axis_index("dp")
    z = lax.axis_index("tensor")
    near = (flip(d, 2), flip(d, 4))
    sib = flip(d, 1)
    cols = wk_ref.shape[1]
    half = depth // 2
    mats = (wk_ref, wv_ref, wq_ref)
    has_left, has_right = z > 0, z < n_z - 1

    barrier = pltpu.get_barrier_semaphore()
    for other in near + (sib,):
        pl.semaphore_signal(barrier, inc=1, device_id=(other, z), device_id_type=MESH)

    @pl.when(has_left)
    def _():
        pl.semaphore_signal(barrier, inc=1, device_id=(d, z - 1), device_id_type=MESH)

    @pl.when(has_right)
    def _():
        pl.semaphore_signal(barrier, inc=1, device_id=(d, z + 1), device_id_type=MESH)

    at_end = (z == 0) | (z == n_z - 1)

    @pl.when(at_end)
    def _():
        pl.semaphore_wait(barrier, 4)

    @pl.when(jnp.logical_not(at_end))
    def _():
        pl.semaphore_wait(barrier, 5)

    def remote(src, dst, send, recv, target):
        return pltpu.make_async_remote_copy(
            src_ref=src,
            dst_ref=dst,
            send_sem=send,
            recv_sem=recv,
            device_id=target,
            device_id_type=MESH,
        )

    def token_copy(way, step):
        src_z = z - step if way == 0 else z + step
        to_z = z + 1 if way == 0 else z - 1
        src = x_ref if step == 0 else xs.at[jnp.clip(src_z, 0, n_z - 1)]
        return remote(
            src,
            xs.at[jnp.clip(src_z, 0, n_z - 1)],
            x_send.at[way, step],
            x_recv.at[way, step],
            (d, jnp.clip(to_z, 0, n_z - 1)),
        )

    def token_sends(way, step):
        if way == 0:
            return (z - step >= 0) & has_right
        return (z + step <= n_z - 1) & has_left

    def token_start(step):
        for way in (0, 1):

            @pl.when(token_sends(way, step))
            def _():
                token_copy(way, step).start()

    def token_wait_recv(step):
        for way in (0, 1):
            arrives = (z - step - 1 >= 0) if way == 0 else (z + step + 1 <= n_z - 1)

            @pl.when(arrives)
            def _():
                src_z = z - step - 1 if way == 0 else z + step + 1
                slot = xs.at[jnp.clip(src_z, 0, n_z - 1)]
                remote(
                    slot, slot, x_send.at[way, step], x_recv.at[way, step], (sib, z)
                ).wait_recv()

    def token_wait_send(step):
        for way in (0, 1):

            @pl.when(token_sends(way, step))
            def _():
                token_copy(way, step).wait_send()

    def block(r, m):
        return ws.at[r, :, pl.ds(m * cols, cols)]

    def part(r, m, h):
        return ws.at[r, pl.ds(h * half, half), pl.ds(m * cols, cols)]

    def own_copy(m, a, h):
        return remote(
            mats[m].at[pl.ds(h * half, half), :],
            part(2 << a, m, h),
            own_send.at[m, a, h],
            own_recv.at[m, a, h],
            (near[a], z),
        )

    def own_start(m):
        for first in (0, 1):
            for a in (0, 1):
                own_copy(m, a, a if first == 0 else 1 - a).start()

    def fwd_copy(m, a):
        h = a
        return remote(
            part(2 << a, m, h),
            part(6, m, h),
            fwd_send.at[m, a],
            fwd_recv.at[m, a],
            (near[1 - a], z),
        )

    def fwd_recv_wait(m, a):
        remote(
            part(6, m, a), part(6, m, a), fwd_send.at[m, a], fwd_recv.at[m, a], (sib, z)
        ).wait_recv()

    def sib_copy(m, j):
        src = mats[m] if j == 0 else block(2 * j, m)
        return remote(src, block(2 * j + 1, m), sib_send.at[m, j], sib_recv.at[m, j], (sib, z))

    def local_copy(m):
        return pltpu.make_async_copy(mats[m], block(0, m), loc_sem.at[m])

    x_local = pltpu.make_async_copy(x_ref, xs.at[z], loc_sem.at[3])

    token_start(0)
    own_start(0)
    own_start(1)
    x_local.start()
    for m in range(3):
        local_copy(m).start()
    for m in range(2):
        sib_copy(m, 0).start()

    def take_own(m):
        for a in (0, 1):
            own_copy(m, a, a).wait_recv()
            fwd_copy(m, a).start()
        for a in (0, 1):
            own_copy(m, a, 1 - a).wait_recv()
            sib_copy(m, a + 1).start()

    def take_diag(m):
        for a in (0, 1):
            fwd_recv_wait(m, a)
        sib_copy(m, 3).start()

    take_own(0)
    own_start(2)
    sib_copy(2, 0).start()
    token_wait_recv(0)
    token_start(1)
    take_own(1)
    take_diag(0)
    token_wait_recv(1)
    token_start(2)
    x_local.wait()
    for m in range(3):
        local_copy(m).wait()
    take_own(2)
    take_diag(1)
    for m in range(2):
        for j in range(4):
            sib_copy(m, j).wait_recv()

    pair = z // 2
    rows = q_ref.shape[0] // 2
    rank = up_ref.shape[1]
    adapter = (1, 2, 0)
    wide = 256

    def slots(side):
        return pl.ds(2 * side, 2)

    def tokens(side, r):
        at = pl.multiple_of(flip(d, r) * depth, 128)
        return xs[slots(side), :, pl.ds(at, depth)].reshape(rows, depth)

    def low(side, m):
        at = din + adapter[m] * rank
        return xs[slots(side), :, at : at + rank].reshape(rows, rank)

    def start_acc(side, m, lo):
        for c in range(0, cols, 128):
            acc[:, lo + c : lo + c + 128] = jnp.dot(
                low(side, m), up_ref[adapter[m], :, c : c + 128], preferred_element_type=F32
            )

    def keys_values(side):
        at_rows = pl.ds(pl.multiple_of(side * rows, rows), rows)
        for m in range(2):
            start_acc(side, m, m * cols)

        def kv_tile(t, carry):
            tile = pl.ds(pl.multiple_of(t * wide, 128), wide)

            def add(r, c):
                acc[:, tile] += jnp.dot(
                    tokens(side, r), ws[r, :, tile], preferred_element_type=F32
                )
                return c

            lax.fori_loop(0, 8, add, 0)
            kv_ref[at_rows, tile] = acc[:, tile].astype(BF)
            return carry

        lax.fori_loop(0, 2 * cols // wide, kv_tile, 0)

    def queries(side):
        at_rows = pl.ds(pl.multiple_of(side * rows, rows), rows)
        start_acc(side, 2, 0)

        def q_add(r, c):
            for lo in range(0, cols, wide):
                width = min(wide, cols - lo)
                acc[:, lo : lo + width] += jnp.dot(
                    tokens(side, r),
                    ws[r, :, 2 * cols + lo : 2 * cols + lo + width],
                    preferred_element_type=F32,
                )
            return c

        lax.fori_loop(0, 8, q_add, 0)
        q_ref[at_rows, :] = acc[:, :cols].astype(BF)

    keys_values(pair)
    take_diag(2)
    for j in range(4):
        sib_copy(2, j).wait_recv()
    queries(pair)
    token_wait_recv(2)
    keys_values(1 - pair)
    queries(1 - pair)

    for step in range(n_z - 1):
        token_wait_send(step)
    for m in range(3):
        for a in (0, 1):
            for h in (0, 1):
                own_copy(m, a, h).wait_send()
            fwd_copy(m, a).wait_send()
        for j in range(4):
            sib_copy(m, j).wait_send()


def project(x, wq, wk, wv, up, n_z, din):
    depth, cols = wk.shape
    rows = n_z * x.shape[0]
    dma = pltpu.SemaphoreType.DMA
    hbm = pl.BlockSpec(memory_space=pl.ANY)
    vmem = pl.BlockSpec(memory_space=pltpu.VMEM)
    return pl.pallas_call(
        functools.partial(project_kernel, depth, n_z, din),
        out_shape=(
            jax.ShapeDtypeStruct((rows, 2 * cols), BF),
            jax.ShapeDtypeStruct((rows, cols), BF),
        ),
        in_specs=[hbm, hbm, hbm, hbm, vmem],
        out_specs=(vmem, vmem),
        scratch_shapes=[
            pltpu.VMEM((n_z,) + x.shape, BF),
            pltpu.VMEM((8, depth, 3 * cols), BF),
            pltpu.VMEM((rows // 2, 2 * cols), F32),
            dma((4,)),
            dma((2, 3)),
            dma((2, 3)),
            dma((3, 2, 2)),
            dma((3, 2, 2)),
            dma((3, 2)),
            dma((3, 2)),
            dma((3, 4)),
            dma((3, 4)),
        ],
        compiler_params=pltpu.CompilerParams(
            collective_id=0, has_side_effects=True, vmem_limit_bytes=60 * 1024 * 1024
        ),
        cost_estimate=pl.CostEstimate(
            flops=6 * rows * din * cols, bytes_accessed=8 * depth * cols * 6, transcendentals=0
        ),
    )(x, wk, wv, wq, up)


epsilon = 1e-05
negative = -1e30


def attend_kernel(live_ref, q_ref, kv_ref, seg_col_ref, seg_row_ref, out_w_ref, out_ref, att):
    rows, cols = q_ref.shape
    count = 128
    live = live_ref[0]
    key_at = lax.broadcasted_iota(jnp.int32, (count, rows), 1)

    @pl.loop(0, rows // count)
    def _(i):
        at = pl.ds(pl.multiple_of(i * count, count), count)
        query_at = i * count + lax.broadcasted_iota(jnp.int32, (count, rows), 0)
        allowed = (
            (seg_col_ref[at, :] == seg_row_ref[...]) & (key_at <= query_at) & (key_at < live)
        )
        for h in range(cols // HD):
            lo = h * HD // 128 * 128
            hi = -(-(h + 1) * HD // 128) * 128
            col = lo + lax.broadcasted_iota(jnp.int32, (count, hi - lo), 1)
            mine = (col >= h * HD) & (col < (h + 1) * HD)
            q = jnp.where(mine, q_ref[at, lo:hi], jnp.zeros((), BF))
            scores = lax.dot_general(
                q, kv_ref[:, lo:hi], (((1,), (1,)), ((), ())), preferred_element_type=F32
            ) / math.sqrt(HD)
            scores = jnp.where(allowed, scores, negative)
            expo = jnp.exp(scores - jnp.max(scores, axis=-1, keepdims=True))
            weights = (expo / jnp.sum(expo, axis=-1, keepdims=True)).astype(BF)
            mixed = jnp.dot(weights, kv_ref[:, cols + lo : cols + hi], preferred_element_type=F32)
            row = i * count + lax.broadcasted_iota(jnp.int32, (count, hi - lo), 0)
            mixed = jnp.where(row < live, mixed, 0.0).astype(BF)
            if h:
                mixed = jnp.where(mine, mixed, att[at, lo:hi])
            att[at, lo:hi] = mixed

    wide = 256

    @pl.loop(0, out_w_ref.shape[1] // wide)
    def _(t):
        tile = pl.ds(pl.multiple_of(t * wide, wide), wide)
        out_ref[:, tile] = jnp.dot(
            att[...], out_w_ref[:, tile], preferred_element_type=F32
        ).astype(BF)


def attend_project(query, stacked, segment, live, out_w):
    rows, cols = query.shape
    vmem = pl.BlockSpec(memory_space=pltpu.VMEM)
    return pl.pallas_call(
        attend_kernel,
        out_shape=jax.ShapeDtypeStruct((rows, out_w.shape[1]), BF),
        in_specs=[pl.BlockSpec(memory_space=pltpu.SMEM)] + [vmem] * 5,
        out_specs=vmem,
        scratch_shapes=[pltpu.VMEM((rows, cols), BF)],
        compiler_params=pltpu.CompilerParams(vmem_limit_bytes=32 * 1024 * 1024),
        cost_estimate=pl.CostEstimate(
            flops=2 * rows * cols * (2 * rows + out_w.shape[1]),
            bytes_accessed=2 * (3 * rows * cols + (cols + rows) * out_w.shape[1]),
            transcendentals=rows * rows * (cols // HD),
        ),
    )(live, query, stacked, segment[:, None], segment[None, :], out_w)


def normalize(hidden_state_input, token_embedding_input, input_norm_gain):
    combined = jnp.concatenate([hidden_state_input, token_embedding_input], 1).astype(jnp.float32)
    factor = lax.rsqrt(jnp.mean(combined * combined, axis=1, keepdims=True) + epsilon)
    return (combined * factor * input_norm_gain).astype(jnp.bfloat16)


def attend_block(query, keys, values, segment, position, live, first, count, key_end):
    heads = query.shape[1] // HD
    block_query = query[first : first + count].reshape(count, heads, HD)
    block_keys = keys.reshape(key_end, heads, HD)
    block_values = values.reshape(key_end, heads, HD)
    scores = jnp.einsum(
        "qhd,khd->hqk", block_query, block_keys, preferred_element_type=jnp.float32
    ) / math.sqrt(HD)
    query_at = position[first : first + count]
    allowed = (
        (segment[first : first + count, None] == segment[None, :key_end])
        & (position[None, :] <= query_at[:, None])
        & (position[None, :] < live)
    )
    scores = jnp.where(allowed[None], scores, negative)
    top = jnp.max(scores, axis=-1, keepdims=True)
    expo = jnp.exp(scores - top)
    weights = (expo / jnp.sum(expo, axis=-1, keepdims=True)).astype(jnp.bfloat16)
    mixed = jnp.einsum("hqk,khd->qhd", weights, block_values, preferred_element_type=jnp.float32)
    mixed = jnp.where((query_at < live)[:, None, None], mixed, 0.0)
    return mixed.astype(jnp.bfloat16).reshape(count, heads * HD)


def body(
    hidden_state_input,
    token_embedding_input,
    input_norm_gain,
    query_projection_weight,
    key_projection_weight,
    value_projection_weight,
    adapter_down_maps,
    adapter_up_maps,
    output_projection_weight,
    segment,
    live_token_length,
    request_cache_row,
):
    adapter_rank_width = adapter_up_maps.shape[1]
    head_cols = query_projection_weight.shape[1]
    normalized_hidden = normalize(hidden_state_input, token_embedding_input, input_norm_gain)
    adapter_update = jnp.dot(
        normalized_hidden, adapter_down_maps, preferred_element_type=jnp.float32
    ).astype(jnp.bfloat16)
    dp, n_z = lax.axis_size("dp"), lax.axis_size("tensor")
    depth = query_projection_weight.shape[0]
    fast = dp == 8 and n_z == 4
    all_rows = lax.all_gather(request_cache_row, "dp", axis=0, tiled=True)
    if fast:
        own = jnp.concatenate([normalized_hidden, adapter_update], 1)
        stacked, query = project(
            own,
            query_projection_weight,
            key_projection_weight,
            value_projection_weight,
            adapter_up_maps,
            n_z,
            dp * depth,
        )
        keys, values = stacked[:, :head_cols], stacked[:, head_cols:]
    else:
        stream_in, stream_low = (
            lax.all_gather(normalized_hidden, "tensor", axis=0, tiled=True),
            lax.all_gather(adapter_update, "tensor", axis=0, tiled=True),
        )
        pieces = (
            lax.all_gather(query_projection_weight, "dp", axis=0, tiled=True),
            lax.all_gather(key_projection_weight, "dp", axis=0, tiled=True),
            lax.all_gather(value_projection_weight, "dp", axis=0, tiled=True),
        )
        folded = tuple(
            (jnp.dot(stream_in, piece, preferred_element_type=jnp.float32) for piece in pieces)
        )
        projected = []
        for adapter_selector in range(3):
            adapter = jnp.dot(
                stream_low[
                    :,
                    adapter_selector * adapter_rank_width : (adapter_selector + 1) * adapter_rank_width,
                ],
                adapter_up_maps[adapter_selector],
                preferred_element_type=jnp.float32,
            )
            projected.append((folded[adapter_selector] + adapter).astype(jnp.bfloat16))
        query, keys, values = projected
        stacked = jnp.concatenate([keys, values], 1)
    stream = query.shape[0]
    position = jnp.arange(stream, dtype=jnp.int32)
    live = live_token_length[0]
    if fast:
        partial = attend_project(
            query, stacked, segment, live_token_length, output_projection_weight
        )
    else:
        block = min(512, stream)
        attended_parts = []
        for block_index in range(stream // block):
            first = block_index * block
            attended_parts.append(
                attend_block(query, keys, values, segment, position, live, first, block, stream)
            )
        attended = jnp.concatenate(attended_parts, 0)
        partial = jnp.dot(
            attended, output_projection_weight, preferred_element_type=jnp.float32
        ).astype(jnp.bfloat16)
    block_out = lax.psum_scatter(partial, "tensor", scatter_dimension=0, tiled=True)
    requests = request_cache_row.shape[0]
    longest = stream // requests
    groups = lax.axis_size("dp")
    piece_len = longest // groups
    numbers = jnp.arange(requests, dtype=jnp.int32)
    membership = ((segment[:, None] == numbers[None, :]) & (position < live)[:, None]).astype(
        jnp.int32
    )
    lengths = jnp.sum(membership, axis=0)
    earlier = numbers[:, None] < numbers[None, :]
    starts = jnp.sum(jnp.where(earlier, lengths[:, None], 0), axis=0)
    offsets = (
        jnp.arange(groups, dtype=jnp.int32)[:, None] * piece_len
        + jnp.arange(piece_len, dtype=jnp.int32)[None, :]
    )
    source_rows = jnp.minimum(starts[None, :, None] + offsets[:, None, :], stream - 1)
    alive_mask = offsets[:, None, :] < lengths[None, :, None]
    taken = jnp.take(stacked, source_rows.reshape(-1), axis=0)
    taken = jnp.where(alive_mask.reshape(-1)[:, None], taken, jnp.zeros((), jnp.bfloat16))
    taken = taken.reshape(groups, requests, piece_len * 2 * head_cols)
    received = lax.all_to_all(taken, "dp", split_axis=0, concat_axis=0, tiled=True)
    total_reqs = groups * requests
    placing = (
        all_rows[:, None] == jnp.arange(total_reqs, dtype=jnp.int32)[None, :]
    ).astype(jnp.bfloat16)
    flat_received = received.reshape(total_reqs, piece_len * 2 * head_cols)
    cache_rows = lax.dot_general(
        placing, flat_received, (((0,), (0,)), ((), ())), preferred_element_type=jnp.float32
    )
    kv_cache = cache_rows.astype(jnp.bfloat16).reshape(total_reqs, piece_len, 2, head_cols)
    return (block_out, kv_cache)


def solution(mesh):
    return jax.shard_map(
        body,
        mesh=mesh,
        in_specs=(
            P(("dp", "tensor"), None),
            P(("dp", "tensor"), None),
            P(),
            P("dp", "tensor"),
            P("dp", "tensor"),
            P("dp", "tensor"),
            P(),
            P(None, None, "tensor"),
            P("tensor", None),
            P("dp"),
            P("dp"),
            P("dp"),
        ),
        out_specs=(P(("dp", "tensor"), None), P(None, "dp", None, "tensor")),
        check_vma=False,
    )
```
